256 devices in a mesh: replica: 16 (over x, z_hi), fsdp: 16 (over z_lo, y, core).
Axes of the slice: x: 4, y: 4, z: 8 (z_hi: 4, z_lo: 2; z = z_hi * 2 + z_lo), core: 2. Of those that a mesh axis runs over, the one named last changes fastest.
Arguments:
- tokens: bfloat16 [16, 8192, 4096], P('replica', 'fsdp'), may hold values from -6 to 6
- kv_cotangent: bfloat16 [16, 8192, 1024], P('replica', 'fsdp'), may hold values from -6 to 6
- inner_weights: bfloat16 [16, 4096, 1024], P('replica', 'fsdp'), may hold values from -0.125 to 0.125
- outer_params: float32 [4096, 1024], P('fsdp', 'replica'), may hold values from -0.09375 to 0.09375
- outer_momentum: float32 [4096, 1024], P('fsdp', 'replica'), may hold values from -0.12 to 0.12
Outputs:
- keys_values: bfloat16 [16, 8192, 1024], P('replica', 'fsdp')
- token_grads: bfloat16 [16, 8192, 4096], P('replica', 'fsdp')
- weight_grads: float32 [16, 4096, 1024], P('replica', 'fsdp')
- new_outer: float32 [4096, 1024], P('fsdp', 'replica')
- new_momentum: float32 [4096, 1024], P('fsdp', 'replica')
- synced_weights: bfloat16 [4096, 1024], P('fsdp')
The draws below stay inside these ranges and needn't reach their ends.
All inputs are finite; a program needn't handle non-finite values.
Results may differ from the reference program's by a relative error of at most 0.013.
Values may be sent and summed in bfloat16 or wider, within the bound.
No kernel may reach another device: no remote copies, remote signals or barrier semaphores. Data moves between devices by JAX's collectives and lax.ppermute only.
A program may use at most 128 MiB of HBM per device.

```python
import jax
import jax.numpy as jnp
from jax import lax

D = 4096
KV = 1024
GROUP_TOK = 8192
N_REPLICA = 16


def spiked(values, rng, source, target, parts, factor):
    def block_of(dim):
        return (jnp.arange(values.shape[dim]) // (values.shape[dim] // parts)).reshape((-1,) + (1,) * (values.ndim - 1 - dim))

    near = jax.random.permutation(rng, parts)[block_of(target)]
    other_side = (block_of(target) + parts // 2) % parts
    return jnp.where((block_of(source) == near) | (block_of(source) == other_side), factor * values, values)


def level_of(stream_key, shape, shards, least, high):
    level, own = 1.0, jax.random.fold_in(stream_key, 6)
    for axis_at, blocks in shards:
        draws = jnp.exp(jax.random.uniform(jax.random.fold_in(own, axis_at), (blocks,), jnp.float32, least / len(shards), high / len(shards)))
        level = level * jnp.repeat(draws, shape[axis_at] // blocks).reshape([-1 if axis == axis_at else 1 for axis in range(len(shape))])
    return level


def gaussian(rng, shape, deviation, limit, shards=(), kind=jnp.bfloat16):
    result = deviation * jax.random.normal(rng, shape, jnp.float32)
    if shards:
        result = result * level_of(rng, shape, shards, -0.22, 0.18)
    return jnp.clip(result, -limit, limit).astype(kind)


def noise_with(stream_key, dims, scale, bound, pieces, heavy, kind=jnp.bfloat16):
    drawn = scale * jax.random.normal(stream_key, dims, jnp.float32)
    if pieces:
        drawn = drawn * level_of(stream_key, dims, pieces, -0.22, 0.18)
    return jnp.clip(spiked(drawn, jax.random.fold_in(stream_key, 3), *heavy), -bound, bound).astype(kind)


def setup_inputs(seed: int = 0) -> dict:
    streams_of = jax.random.split(jax.random.key(seed), 6)
    return {
        "tokens": noise_with(streams_of[0], (N_REPLICA, GROUP_TOK, D), 1.0, 6.0, ((0, 16), (1, 16)), (1, 2, 16, 2.0)),
        "kv_cotangent": gaussian(streams_of[1], (N_REPLICA, GROUP_TOK, KV), 1.0, 6.0, ((0, 16), (1, 16))),
        "inner_weights": noise_with(streams_of[2], (N_REPLICA, D, KV), D ** -0.5, 0.125, ((0, 16), (1, 16)), (0, 2, 16, 2.0)),
        "outer_params": gaussian(streams_of[3], (D, KV), D ** -0.5, 0.09375, ((0, 16), (1, 16)), jnp.float32),
        "outer_momentum": gaussian(streams_of[4], (D, KV), 0.02, 0.12, ((0, 16), (1, 16)), jnp.float32),
    }


def one_replica(items):
    rows_in, cot_in, w_in = items
    values = jnp.dot(rows_in, w_in, preferred_element_type=jnp.float32).astype(jnp.bfloat16)
    back = lax.dot_general(cot_in, w_in, (((1,), (1,)), ((), ())), preferred_element_type=jnp.float32).astype(jnp.bfloat16)
    grads = lax.dot_general(rows_in, cot_in, (((0,), (0,)), ((), ())), preferred_element_type=jnp.float32)
    return values, back, grads


def reference(tokens, kv_cotangent, inner_weights, outer_params, outer_momentum):
    keys_values, token_grads, weight_grads = lax.map(one_replica, (tokens, kv_cotangent, inner_weights))
    mean_inner = jnp.sum(inner_weights.astype(jnp.float32), axis=0) / N_REPLICA
    pseudo = outer_params - mean_inner
    new_momentum = 0.9 * outer_momentum + pseudo
    new_outer = outer_params - 0.7 * (pseudo + 0.9 * new_momentum)
    synced_weights = new_outer.astype(jnp.bfloat16)
    return keys_values, token_grads, weight_grads, new_outer, new_momentum, synced_weights
```

```python
import functools

import jax
import jax.numpy as jnp
from jax import lax
from jax.experimental import pallas as pl
from jax.experimental.pallas import tpu as pltpu
from jax.sharding import PartitionSpec as P

NZ, NY, NC = 2, 4, 2
NX, NH = 4, 4
F32, BF16 = jnp.float32, jnp.bfloat16
VMEM_LIMIT = 60 * 1024 * 1024


def shift_fsdp(a, dz=0, dy=0, dc=0):
    pairs = []
    for z in range(NZ):
        for y in range(NY):
            for c in range(NC):
                to = (((z + dz) % NZ) * NY + (y + dy) % NY) * NC + (c + dc) % NC
                pairs.append(((z * NY + y) * NC + c, to))
    return lax.ppermute(a, "fsdp", pairs)


ANY = pl.BlockSpec(memory_space=pl.ANY)
SMEM = pl.BlockSpec(memory_space=pltpu.SMEM)


def place(me):
    return me // (NC * NY), (me // NC) % NY, me % NC


def block_at(z, y, c):
    return (z * NY + y) * NC + c


def columns(ref, b, width=256):
    return ref.at[:, pl.ds(pl.multiple_of(b * width, width), width)]


GRAD_DIMS = (((0,), (0,)), ((), ()))


def far_gradients(here, tok, tok_rx, cot, cot_rx, after):
    rows, kv = cot.shape

    def y_of(i, here):
        step = jnp.where(i == 0, 2, jnp.where(i == 1, 1, jnp.where(i == 2, 3, 0)))
        return (place(here[0])[1] + step) % NY

    def own_block(i, here):
        z, _, core = place(here[0])
        return 0, block_at(1 - z, y_of(i, here), core)

    def body(here_ref, t_ref, tr_ref, c_ref, cr_ref, *rest):
        a_ref, b_ref, d_ref = rest[len(after) :]
        i = pl.program_id(0)
        acc = lax.dot_general(t_ref[...], c_ref[...], GRAD_DIMS, preferred_element_type=F32)
        acc += lax.dot_general(tr_ref[...], cr_ref[...], GRAD_DIMS, preferred_element_type=F32)
        acc = acc.astype(BF16)

        @pl.when(i == 0)
        def _():
            a_ref[...] = acc

        @pl.when((i == 1) | (i == 2))
        def _():
            b_ref[...] = acc

        @pl.when(i == 3)
        def _():
            d_ref[...] = acc

    return pl.pallas_call(
        body,
        grid_spec=pltpu.PrefetchScalarGridSpec(
            num_scalar_prefetch=1,
            grid=(NY,),
            in_specs=[
                pl.BlockSpec((rows, 256), own_block),
                pl.BlockSpec((rows, 256), own_block),
                pl.BlockSpec((rows, kv), lambda i, here: (0, 0)),
                pl.BlockSpec((rows, kv), lambda i, here: (0, 0)),
            ]
            + [ANY] * len(after),
            out_specs=[
                pl.BlockSpec((256, kv), lambda i, here: (0, 0)),
                pl.BlockSpec((256, kv), lambda i, here: (jnp.clip(i - 1, 0, 1), 0)),
                pl.BlockSpec((256, kv), lambda i, here: (0, 0)),
            ],
        ),
        out_shape=[jax.ShapeDtypeStruct((m * 256, kv), BF16) for m in (1, 2, 1)],
        compiler_params=pltpu.CompilerParams(vmem_limit_bytes=VMEM_LIMIT),
        name="far_gradients",
    )(here, tok, tok_rx, cot, cot_rx, *after)


def add_blocks(own, jobs, dtype, after=(), along=()):
    kv = own.shape[1]
    flat = [(own, k, m) for m, (k, _) in enumerate(jobs)]
    flat += [(a, k, m) for m, (_, others) in enumerate(jobs) for a, k in others]
    n_in = len(flat) + len(after) + len(along)

    def body(*refs):
        ins, outs = refs[: len(flat)], refs[n_in : n_in + len(jobs)]
        for m, o in enumerate(outs):
            acc = ins[m][...]
            for ref, (_, _, job) in zip(ins[len(jobs) :], flat[len(jobs) :]):
                if job == m:
                    acc = acc + ref[...].astype(F32)
            o[...] = acc.astype(dtype)

    def spec(k):
        return pl.BlockSpec((256, kv), lambda i: (k, 0))

    return pl.pallas_call(
        body,
        grid=(1,),
        in_specs=[spec(k) for _, k, _ in flat] + [ANY] * (len(after) + len(along)),
        out_specs=[spec(0) for _ in jobs] + [ANY] * len(along),
        out_shape=[jax.ShapeDtypeStruct((256, kv), dtype) for _ in jobs]
        + [jax.ShapeDtypeStruct(a.shape, a.dtype) for a in along],
        input_output_aliases={len(flat) + len(after) + k: len(jobs) + k for k in range(len(along))},
        compiler_params=pltpu.CompilerParams(vmem_limit_bytes=VMEM_LIMIT),
        name="add_blocks",
    )(*[a for a, _, _ in flat], *after, *along)


def project(here, tok, tok_rx, cot, cot_rx, pieces, steps, before=None, after=()):
    rows, d = tok.shape
    kv = cot.shape[1]
    far = before is not None
    n_w = len(pieces)
    deep = NY * 256

    def body(here_ref, t_ref, tx_ref, c_ref, cx_ref, *rest):
        w_refs, rest = rest[:n_w], rest[n_w:]
        if far:
            own_in, send_in = rest[:2]
            rest = rest[4 + len(after) :]
            own_ref, tg_ref, out_ref = rest[:3]
            w_v, t_v, tr_v, c_v, cr_v, g_v, own_v, send_v, out_v, sems = rest[3:]
        else:
            rest = rest[len(after) :]
            own_ref, tg_ref, out_ref, send_ref, grad_ref = rest[:5]
            w_v, t_v, tr_v, c_v, cr_v, g_v, own_v, send_v, out_v, grad_v, sems = rest[5:]
        z, y, core = place(here_ref[0])
        zz = 1 - z if far else z
        ys = [(y + step) % NY for step in steps]
        count = [0]

        def copy(src, dst):
            c = pltpu.make_async_copy(src, dst, sems.at[count[0]])
            count[0] += 1
            c.start()
            return c

        ready_c = copy(c_ref, c_v)
        ready_w = [copy(r, w_v.at[pl.ds(k * 256, 256)]) for k, r in enumerate(w_refs)]
        ready_t = [copy(columns(t_ref, block_at(zz, yy, core)), columns(t_v, k)) for k, yy in enumerate(ys)]
        ready_cr = copy(cx_ref, cr_v)
        ready_tr = [copy(columns(tx_ref, block_at(zz, yy, core)), columns(tr_v, k)) for k, yy in enumerate(ys)]
        if far:
            ready_own = copy(own_in, own_v)
            ready_send = copy(send_in, send_v)
        done = []
        trans = (((1,), (1,)), ((), ()))
        ready_c.wait()
        for k in range(NY):
            ready_w[k].wait()
            at = slice(k * 256, k * 256 + 256)
            g_v[:, at] = lax.dot_general(
                c_v[...], w_v[at, :], trans, preferred_element_type=F32
            ).astype(BF16)
            done.append(copy(columns(g_v, k), columns(tg_ref, block_at(zz, ys[k], core))))
        for c in ready_t:
            c.wait()
        sums = jnp.dot(t_v[...], w_v[...], preferred_element_type=F32)
        if far:
            ready_own.wait()
            sums += own_v[...]
        own_v[...] = sums
        done.append(copy(own_v, own_ref))
        ready_cr.wait()
        out_v[:, :deep] = lax.dot_general(
            cr_v[...], w_v[...], trans, preferred_element_type=F32
        ).astype(BF16)
        for c in ready_tr:
            c.wait()
        sums = jnp.dot(tr_v[...], w_v[...], preferred_element_type=F32)
        if far:
            ready_send.wait()
            out_v[:, deep:] = (send_v[...] + sums).astype(BF16)
            done.append(copy(out_v, out_ref.at[:, pl.ds(deep, deep + kv)]))
        else:
            done.append(copy(out_v, out_ref.at[:, pl.ds(0, deep)]))
            send_v[...] = sums
            done.append(copy(send_v, send_ref))
            for k in range(NY):
                at = slice(k * 256, k * 256 + 256)
                acc = lax.dot_general(t_v[:, at], c_v[...], GRAD_DIMS, preferred_element_type=F32)
                acc += lax.dot_general(tr_v[:, at], cr_v[...], GRAD_DIMS, preferred_element_type=F32)
                grad_v[at, :] = acc
                done.append(copy(grad_v.at[pl.ds(k * 256, 256)], grad_ref.at[pl.ds(k * 256, 256)]))
        for c in done:
            c.wait()

    sums = jax.ShapeDtypeStruct((rows, kv), F32)
    out_shape = [
        sums,
        jax.ShapeDtypeStruct((rows, d), BF16),
        jax.ShapeDtypeStruct((rows, 2 * deep + kv), BF16),
    ]
    args = [here, tok, tok_rx, cot, cot_rx, *pieces]
    alias = {}
    scratch = [
        pltpu.VMEM((deep, kv), BF16),
        pltpu.VMEM((rows, deep), BF16),
        pltpu.VMEM((rows, deep), BF16),
        pltpu.VMEM((rows, kv), BF16),
        pltpu.VMEM((rows, kv), BF16),
        pltpu.VMEM((rows, deep), BF16),
        pltpu.VMEM((rows, kv), F32),
        pltpu.VMEM((rows, kv), F32),
        pltpu.VMEM((rows, deep + (kv if far else 0)), BF16),
    ]
    if far:
        own, send, grads_in, out_in = before
        alias = {len(args) + 2: 1, len(args) + 3: 2}
        args += [own, send, grads_in, out_in]
    else:
        gradient = jax.ShapeDtypeStruct((deep, kv), F32)
        out_shape += [sums, gradient]
        scratch.append(pltpu.VMEM(gradient.shape, F32))
    args += list(after)
    return pl.pallas_call(
        body,
        in_specs=[SMEM] + [ANY] * (len(args) - 1),
        out_specs=[ANY] * len(out_shape),
        out_shape=out_shape,
        scratch_shapes=scratch + [pltpu.SemaphoreType.DMA((32,))],
        input_output_aliases=alias,
        compiler_params=pltpu.CompilerParams(vmem_limit_bytes=VMEM_LIMIT),
        name="project",
    )(*args)


def merge(here, own, other_rx, grads, steps, after):
    rows, kv = own.shape
    deep = NY * 256

    def body(here_ref, own_ref, a_ref, _, *rest):
        kv_ref, tg_ref, own_v, a_v, kv_v, sems = rest[len(after) :]
        z, y, core = place(here_ref[0])
        count = [0]

        def copy(src, dst):
            c = pltpu.make_async_copy(src, dst, sems.at[count[0]])
            count[0] += 1
            c.start()
            return c

        load_kv = copy(a_ref.at[:, pl.ds(2 * deep, kv)], a_v.at[:, pl.ds(2 * deep, kv)])
        load_own = copy(own_ref, own_v)
        loads = [copy(columns(a_ref, k), columns(a_v, k)) for k in range(2 * NY)]
        out = []
        for k, load in enumerate(loads):
            load.wait()
            zz = z if k < NY else 1 - z
            at = block_at(zz, (y + steps[k % NY]) % NY, 1 - core)
            out.append(copy(columns(a_v, k), columns(tg_ref, at)))
        load_kv.wait()
        load_own.wait()
        kv_v[...] = (own_v[...] + a_v[:, 2 * deep :].astype(F32)).astype(BF16)
        out.append(copy(kv_v, kv_ref))
        for c in out:
            c.wait()

    return pl.pallas_call(
        body,
        in_specs=[SMEM] + [ANY] * (3 + len(after)),
        out_specs=[ANY, ANY],
        out_shape=[
            jax.ShapeDtypeStruct((rows, kv), BF16),
            jax.ShapeDtypeStruct(grads.shape, BF16),
        ],
        scratch_shapes=[
            pltpu.VMEM((rows, kv), F32),
            pltpu.VMEM(other_rx.shape, BF16),
            pltpu.VMEM((rows, kv), BF16),
            pltpu.SemaphoreType.DMA((4 * NY + 3,)),
        ],
        input_output_aliases={3: 1},
        compiler_params=pltpu.CompilerParams(vmem_limit_bytes=VMEM_LIMIT),
        name="merge",
    )(here, own, other_rx, grads, *after)


WHOLE = pl.BlockSpec(memory_space=pltpu.VMEM)


def shift_replica(a, dx=0, dh=0):
    pairs = [
        (x * NH + h, ((x + dx) % NX) * NH + (h + dh) % NH) for x in range(NX) for h in range(NH)
    ]
    return lax.ppermute(a, "replica", pairs)


def small_call(body, n_in, after, out_shape, scratch, name):
    return pl.pallas_call(
        body,
        in_specs=[SMEM] + [WHOLE] * n_in + [ANY] * len(after),
        out_specs=[WHOLE] * len(out_shape),
        out_shape=out_shape,
        scratch_shapes=scratch,
        compiler_params=pltpu.CompilerParams(vmem_limit_bytes=VMEM_LIMIT),
        name=name,
    )


X_GROUPS = [[x * NH + h for x in range(NX)] for h in range(NH)]
H_GROUPS = [[x * NH + h for h in range(NH)] for x in range(NX)]


def sum_along_x(here, parts, after):
    _, rows, wide = parts.shape
    thin = wide // NH

    def body(here_ref, p_ref, *rest):
        out_ref = rest[len(after)]
        acc = p_ref[0].astype(F32)
        for k in range(1, NX):
            acc += p_ref[k].astype(F32)
        out_ref[...] = acc.T.astype(BF16).reshape(NH, thin, rows)

    out = [jax.ShapeDtypeStruct((NH, thin, rows), BF16)]
    return small_call(body, 1, after, out, [], "sum_along_x")(here, parts, *after)[0]


def outer_step(here, parts, params, moment, after):
    def body(here_ref, t_ref, p_ref, m_ref, *rest):
        np_ref, nm_ref, s_ref = rest[len(after) :]
        total = t_ref[0].astype(F32)
        for k in range(1, NH):
            total += t_ref[k].astype(F32)
        p = p_ref[...]
        pseudo = p - total / (NX * NH)
        nm = 0.9 * m_ref[...] + pseudo
        new = p - 0.7 * (pseudo + 0.9 * nm)
        nm_ref[...] = nm
        np_ref[...] = new
        s_ref[...] = new.astype(BF16)

    out = [jax.ShapeDtypeStruct(params.shape, d) for d in (F32, F32, BF16)]
    return small_call(body, 3, after, out, [], "outer_step")(here, parts, params, moment, *after)


def join_h(here, parts, after):
    thin, rows = parts[0].shape

    def body(here_ref, *rest):
        part_refs, out_ref, total = rest[:NH], rest[-2], rest[-1]
        h = here_ref[1] % NH
        for k in range(NH):
            at = pl.multiple_of(((h + NH - k) % NH) * thin, thin)
            total[pl.ds(at, thin), :] = part_refs[k][...].astype(F32)
        out_ref[...] = total[...].T.astype(BF16)

    return small_call(
        body,
        NH,
        after,
        [jax.ShapeDtypeStruct((rows, NH * thin), BF16)],
        [pltpu.VMEM((NH * thin, rows), F32)],
        "join_h",
    )(here, *parts, *after)[0]


def join_x(here, parts, after):
    rows, wide = parts[0].shape

    def body(here_ref, *rest):
        part_refs, out_ref, sems = rest[:NX], rest[-2], rest[-1]
        x = here_ref[1] // NH
        copies = [
            pltpu.make_async_copy(
                part_refs[k], columns(out_ref, (x + NX - k) % NX, wide), sems.at[k]
            )
            for k in range(NX)
        ]
        for c in copies:
            c.start()
        for c in copies:
            c.wait()

    return pl.pallas_call(
        body,
        in_specs=[SMEM] + [WHOLE] * NX + [ANY] * len(after),
        out_specs=ANY,
        out_shape=jax.ShapeDtypeStruct((rows, NX * wide), BF16),
        scratch_shapes=[pltpu.SemaphoreType.DMA((NX,))],
        compiler_params=pltpu.CompilerParams(vmem_limit_bytes=VMEM_LIMIT),
        name="join_x",
    )(here, *parts, *after)


def on_device(tokens, kv_cotangent, inner_weights, outer_params, outer_momentum):
    tok, cot, w = tokens[0], kv_cotangent[0], inner_weights[0]
    here = jnp.stack([lax.axis_index(a).astype(jnp.int32) for a in ("fsdp", "replica")])

    w_dn = shift_fsdp(w, dy=1)
    w_up = shift_fsdp(w, dy=-1)
    w_z = shift_fsdp(w, dz=1)

    tok_rx = shift_fsdp(tok, dc=1)
    cot_rx = shift_fsdp(cot, dc=1)

    parts = w.reshape(w.shape[0], NX, w.shape[1] // NX).transpose(1, 0, 2)
    parts = lax.all_to_all(parts, "replica", 0, 0, axis_index_groups=X_GROUPS, tiled=True)
    sum_x = sum_along_x(here, parts, ())

    w_op = shift_fsdp(w_dn, dy=1)
    wz_up = shift_fsdp(w_z, dy=-1)
    wz_dn = shift_fsdp(w_z, dy=1)
    wz_op = shift_fsdp(wz_up, dy=-1)

    g1, g2, g3 = far_gradients(here, tok, tok_rx, cot, cot_rx, (sum_x, w_dn, w_up, w_z))
    r1 = shift_fsdp(g1, dz=1)
    r2 = shift_fsdp(g2, dz=1)
    r3 = shift_fsdp(g3, dz=1)

    steps = (0, NY - 1, 1, 2)
    kv_own, grads, to_core, kv_send, own = project(
        here, tok, tok_rx, cot, cot_rx, [w, w_dn, w_up, w_op], steps, after=(g1,)
    )

    to_up, sum_x = add_blocks(own, [(3, [(r1, 0)])], BF16, along=(sum_x,))
    total = lax.all_to_all(sum_x, "replica", 0, 0, axis_index_groups=H_GROUPS, tiled=True)
    two_down = shift_fsdp(to_up, dy=1)

    to_up, to_dn = add_blocks(
        own, [(2, [(r2, 0), (two_down, 0)]), (1, [(r2, 1)])], BF16, ()
    )
    from_dn = shift_fsdp(to_up, dy=1)
    from_up = shift_fsdp(to_dn, dy=-1)

    new_params, new_moment, synced = outer_step(
        here, total, outer_params.T, outer_momentum.T, (to_up,)
    )
    synced = [synced] + [shift_replica(synced, dh=k) for k in range(1, NH)]
    kv_own, grads, to_core = project(
        here,
        tok,
        tok_rx,
        cot,
        cot_rx,
        [w_z, wz_dn, wz_up, wz_op],
        steps,
        (kv_own, kv_send, grads, to_core),
        after=(synced[0],),
    )
    other_rx = shift_fsdp(to_core, dc=1)
    keys_values, token_grads = merge(here, kv_own, other_rx, grads, steps, (kv_own,))
    synced = join_h(here, synced, (keys_values,))
    synced = [synced] + [shift_replica(synced, dx=k) for k in range(1, NX)]
    (weight_grads,) = add_blocks(
        own, [(0, [(r3, 0), (from_dn, 0), (from_up, 0)])], F32, (synced[0],)
    )
    synced = join_x(here, synced, (weight_grads,))

    return (
        keys_values[None],
        token_grads[None],
        weight_grads[None],
        new_params.T,
        new_moment.T,
        synced,
    )


def solution(mesh):
    return jax.shard_map(
        on_device,
        mesh=mesh,
        in_specs=(
            P("replica", "fsdp", None),
            P("replica", "fsdp", None),
            P("replica", "fsdp", None),
            P("fsdp", "replica"),
            P("fsdp", "replica"),
        ),
        out_specs=(
            P("replica", "fsdp", None),
            P("replica", "fsdp", None),
            P("replica", "fsdp", None),
            P("fsdp", "replica"),
            P("fsdp", "replica"),
            P("fsdp", None),
        ),
        check_vma=False,
    )
```

```python
import functools

import jax
import jax.numpy as jnp
from jax import lax
from jax.experimental import pallas as pl
from jax.experimental.pallas import tpu as pltpu
from jax.sharding import PartitionSpec as P

NZ, NY, NC = 2, 4, 2
NX, NH = 4, 4
F32, BF16 = jnp.float32, jnp.bfloat16
VMEM_LIMIT = 60 * 1024 * 1024


def shift_fsdp(a, dz=0, dy=0, dc=0):
    pairs = []
    for z in range(NZ):
        for y in range(NY):
            for c in range(NC):
                to = (((z + dz) % NZ) * NY + (y + dy) % NY) * NC + (c + dc) % NC
                pairs.append(((z * NY + y) * NC + c, to))
    return lax.ppermute(a, "fsdp", pairs)


ANY = pl.BlockSpec(memory_space=pl.ANY)
SMEM = pl.BlockSpec(memory_space=pltpu.SMEM)


def place(me):
    return me // (NC * NY), (me // NC) % NY, me % NC


def block_at(z, y, c):
    return (z * NY + y) * NC + c


def columns(ref, b, width=256):
    return ref.at[:, pl.ds(pl.multiple_of(b * width, width), width)]


GRAD_DIMS = (((0,), (0,)), ((), ()))


def far_gradients(here, tok, tok_rx, cot, cot_rx, after):
    rows, kv = cot.shape

    def y_of(i, here):
        step = jnp.where(i == 0, 2, jnp.where(i == 1, 1, jnp.where(i == 2, 3, 0)))
        return (place(here[0])[1] + step) % NY

    def own_block(i, here):
        z, _, core = place(here[0])
        return 0, block_at(1 - z, y_of(i, here), core)

    def body(here_ref, t_ref, tr_ref, c_ref, cr_ref, *rest):
        a_ref, b_ref, d_ref = rest[len(after) :]
        i = pl.program_id(0)
        acc = lax.dot_general(t_ref[...], c_ref[...], GRAD_DIMS, preferred_element_type=F32)
        acc += lax.dot_general(tr_ref[...], cr_ref[...], GRAD_DIMS, preferred_element_type=F32)
        acc = acc.astype(BF16)

        @pl.when(i == 0)
        def _():
            a_ref[...] = acc

        @pl.when((i == 1) | (i == 2))
        def _():
            b_ref[...] = acc

        @pl.when(i == 3)
        def _():
            d_ref[...] = acc

    return pl.pallas_call(
        body,
        grid_spec=pltpu.PrefetchScalarGridSpec(
            num_scalar_prefetch=1,
            grid=(NY,),
            in_specs=[
                pl.BlockSpec((rows, 256), own_block),
                pl.BlockSpec((rows, 256), own_block),
                pl.BlockSpec((rows, kv), lambda i, here: (0, 0)),
                pl.BlockSpec((rows, kv), lambda i, here: (0, 0)),
            ]
            + [ANY] * len(after),
            out_specs=[
                pl.BlockSpec((256, kv), lambda i, here: (0, 0)),
                pl.BlockSpec((256, kv), lambda i, here: (jnp.clip(i - 1, 0, 1), 0)),
                pl.BlockSpec((256, kv), lambda i, here: (0, 0)),
            ],
        ),
        out_shape=[jax.ShapeDtypeStruct((m * 256, kv), BF16) for m in (1, 2, 1)],
        compiler_params=pltpu.CompilerParams(vmem_limit_bytes=VMEM_LIMIT),
        name="far_gradients",
    )(here, tok, tok_rx, cot, cot_rx, *after)


def add_blocks(own, jobs, dtype, after=(), along=()):
    kv = own.shape[1]
    flat = [(own, k, m) for m, (k, _) in enumerate(jobs)]
    flat += [(a, k, m) for m, (_, others) in enumerate(jobs) for a, k in others]
    n_in = len(flat) + len(after) + len(along)

    def body(*refs):
        ins, outs = refs[: len(flat)], refs[n_in : n_in + len(jobs)]
        for m, o in enumerate(outs):
            acc = ins[m][...]
            for ref, (_, _, job) in zip(ins[len(jobs) :], flat[len(jobs) :]):
                if job == m:
                    acc = acc + ref[...].astype(F32)
            o[...] = acc.astype(dtype)

    def spec(k):
        return pl.BlockSpec((256, kv), lambda i: (k, 0))

    return pl.pallas_call(
        body,
        grid=(1,),
        in_specs=[spec(k) for _, k, _ in flat] + [ANY] * (len(after) + len(along)),
        out_specs=[spec(0) for _ in jobs] + [ANY] * len(along),
        out_shape=[jax.ShapeDtypeStruct((256, kv), dtype) for _ in jobs]
        + [jax.ShapeDtypeStruct(a.shape, a.dtype) for a in along],
        input_output_aliases={len(flat) + len(after) + k: len(jobs) + k for k in range(len(along))},
        compiler_params=pltpu.CompilerParams(vmem_limit_bytes=VMEM_LIMIT),
        name="add_blocks",
    )(*[a for a, _, _ in flat], *after, *along)


def project(here, tok, tok_rx, cot, cot_rx, pieces, steps, before=None, after=()):
    rows, d = tok.shape
    kv = cot.shape[1]
    far = before is not None
    n_w = len(pieces)
    deep = NY * 256

    def body(here_ref, t_ref, tx_ref, c_ref, cx_ref, *rest):
        w_refs, rest = rest[:n_w], rest[n_w:]
        if far:
            own_in, send_in = rest[:2]
            rest = rest[4 + len(after) :]
            own_ref, tg_ref, out_ref = rest[:3]
            w_v, t_v, tr_v, c_v, cr_v, g_v, own_v, send_v, out_v, sems = rest[3:]
        else:
            rest = rest[len(after) :]
            own_ref, tg_ref, out_ref, send_ref, grad_ref = rest[:5]
            w_v, t_v, tr_v, c_v, cr_v, g_v, own_v, send_v, out_v, grad_v, sems = rest[5:]
        z, y, core = place(here_ref[0])
        zz = 1 - z if far else z
        ys = [(y + step) % NY for step in steps]
        count = [0]

        def copy(src, dst):
            c = pltpu.make_async_copy(src, dst, sems.at[count[0]])
            count[0] += 1
            c.start()
            return c

        ready_c = copy(c_ref, c_v)
        ready_w = [copy(r, w_v.at[pl.ds(k * 256, 256)]) for k, r in enumerate(w_refs)]
        ready_t = [copy(columns(t_ref, block_at(zz, yy, core)), columns(t_v, k)) for k, yy in enumerate(ys)]
        ready_cr = copy(cx_ref, cr_v)
        ready_tr = [copy(columns(tx_ref, block_at(zz, yy, core)), columns(tr_v, k)) for k, yy in enumerate(ys)]
        if far:
            ready_own = copy(own_in, own_v)
            ready_send = copy(send_in, send_v)
        done = []
        trans = (((1,), (1,)), ((), ()))
        ready_c.wait()
        for k in range(NY):
            ready_w[k].wait()
            at = slice(k * 256, k * 256 + 256)
            g_v[:, at] = lax.dot_general(
                c_v[...], w_v[at, :], trans, preferred_element_type=F32
            ).astype(BF16)
            done.append(copy(columns(g_v, k), columns(tg_ref, block_at(zz, ys[k], core))))
        for c in ready_t:
            c.wait()
        sums = jnp.dot(t_v[...], w_v[...], preferred_element_type=F32)
        if far:
            ready_own.wait()
            sums += own_v[...]
        own_v[...] = sums
        done.append(copy(own_v, own_ref))
        ready_cr.wait()
        out_v[:, :deep] = lax.dot_general(
            cr_v[...], w_v[...], trans, preferred_element_type=F32
        ).astype(BF16)
        for c in ready_tr:
            c.wait()
        sums = jnp.dot(tr_v[...], w_v[...], preferred_element_type=F32)
        if far:
            ready_send.wait()
            out_v[:, deep:] = (send_v[...] + sums).astype(BF16)
            done.append(copy(out_v, out_ref.at[:, pl.ds(deep, deep + kv)]))
        else:
            done.append(copy(out_v, out_ref.at[:, pl.ds(0, deep)]))
            send_v[...] = sums
            done.append(copy(send_v, send_ref))
            for k in range(NY):
                at = slice(k * 256, k * 256 + 256)
                acc = lax.dot_general(t_v[:, at], c_v[...], GRAD_DIMS, preferred_element_type=F32)
                acc += lax.dot_general(tr_v[:, at], cr_v[...], GRAD_DIMS, preferred_element_type=F32)
                grad_v[at, :] = acc
                done.append(copy(grad_v.at[pl.ds(k * 256, 256)], grad_ref.at[pl.ds(k * 256, 256)]))
        for c in done:
            c.wait()

    sums = jax.ShapeDtypeStruct((rows, kv), F32)
    out_shape = [
        sums,
        jax.ShapeDtypeStruct((rows, d), BF16),
        jax.ShapeDtypeStruct((rows, 2 * deep + kv), BF16),
    ]
    args = [here, tok, tok_rx, cot, cot_rx, *pieces]
    alias = {}
    scratch = [
        pltpu.VMEM((deep, kv), BF16),
        pltpu.VMEM((rows, deep), BF16),
        pltpu.VMEM((rows, deep), BF16),
        pltpu.VMEM((rows, kv), BF16),
        pltpu.VMEM((rows, kv), BF16),
        pltpu.VMEM((rows, deep), BF16),
        pltpu.VMEM((rows, kv), F32),
        pltpu.VMEM((rows, kv), F32),
        pltpu.VMEM((rows, deep + (kv if far else 0)), BF16),
    ]
    if far:
        own, send, grads_in, out_in = before
        alias = {len(args) + 2: 1, len(args) + 3: 2}
        args += [own, send, grads_in, out_in]
    else:
        gradient = jax.ShapeDtypeStruct((deep, kv), F32)
        out_shape += [sums, gradient]
        scratch.append(pltpu.VMEM(gradient.shape, F32))
    args += list(after)
    return pl.pallas_call(
        body,
        in_specs=[SMEM] + [ANY] * (len(args) - 1),
        out_specs=[ANY] * len(out_shape),
        out_shape=out_shape,
        scratch_shapes=scratch + [pltpu.SemaphoreType.DMA((32,))],
        input_output_aliases=alias,
        compiler_params=pltpu.CompilerParams(vmem_limit_bytes=VMEM_LIMIT),
        name="project",
    )(*args)


def merge(here, own, other_rx, grads, steps, after):
    rows, kv = own.shape
    deep = NY * 256

    def body(here_ref, own_ref, a_ref, _, *rest):
        kv_ref, tg_ref, own_v, a_v, kv_v, sems = rest[len(after) :]
        z, y, core = place(here_ref[0])
        count = [0]

        def copy(src, dst):
            c = pltpu.make_async_copy(src, dst, sems.at[count[0]])
            count[0] += 1
            c.start()
            return c

        load_kv = copy(a_ref.at[:, pl.ds(2 * deep, kv)], a_v.at[:, pl.ds(2 * deep, kv)])
        load_own = copy(own_ref, own_v)
        loads = [copy(columns(a_ref, k), columns(a_v, k)) for k in range(2 * NY)]
        out = []
        for k, load in enumerate(loads):
            load.wait()
            zz = z if k < NY else 1 - z
            at = block_at(zz, (y + steps[k % NY]) % NY, 1 - core)
            out.append(copy(columns(a_v, k), columns(tg_ref, at)))
        load_kv.wait()
        load_own.wait()
        kv_v[...] = (own_v[...] + a_v[:, 2 * deep :].astype(F32)).astype(BF16)
        out.append(copy(kv_v, kv_ref))
        for c in out:
            c.wait()

    return pl.pallas_call(
        body,
        in_specs=[SMEM] + [ANY] * (3 + len(after)),
        out_specs=[ANY, ANY],
        out_shape=[
            jax.ShapeDtypeStruct((rows, kv), BF16),
            jax.ShapeDtypeStruct(grads.shape, BF16),
        ],
        scratch_shapes=[
            pltpu.VMEM((rows, kv), F32),
            pltpu.VMEM(other_rx.shape, BF16),
            pltpu.VMEM((rows, kv), BF16),
            pltpu.SemaphoreType.DMA((4 * NY + 3,)),
        ],
        input_output_aliases={3: 1},
        compiler_params=pltpu.CompilerParams(vmem_limit_bytes=VMEM_LIMIT),
        name="merge",
    )(here, own, other_rx, grads, *after)


WHOLE = pl.BlockSpec(memory_space=pltpu.VMEM)


def small_call(body, n_in, after, out_shape, scratch, name):
    return pl.pallas_call(
        body,
        in_specs=[SMEM] + [WHOLE] * n_in + [ANY] * len(after),
        out_specs=[WHOLE] * len(out_shape),
        out_shape=out_shape,
        scratch_shapes=scratch,
        compiler_params=pltpu.CompilerParams(vmem_limit_bytes=VMEM_LIMIT),
        name=name,
    )


X_GROUPS = [[x * NH + h for x in range(NX)] for h in range(NH)]
H_GROUPS = [[x * NH + h for h in range(NH)] for x in range(NX)]


def sum_along_h(here, parts, after):
    _, wide, rows = parts.shape

    def body(here_ref, p_ref, *rest):
        out_ref = rest[len(after)]
        acc = p_ref[0].astype(F32)
        for k in range(1, NH):
            acc += p_ref[k].astype(F32)
        out_ref[...] = acc.astype(BF16).reshape(out_ref.shape)

    out = [jax.ShapeDtypeStruct((NX, wide // NX, rows), BF16)]
    return small_call(body, 1, after, out, [], "sum_along_h")(here, parts, *after)[0]


def outer_step(here, parts, params, moment, after):
    def body(here_ref, t_ref, p_ref, m_ref, *rest):
        np_ref, nm_ref, s_ref = rest[len(after) :]
        total = t_ref[0].astype(F32)
        for k in range(1, NX):
            total += t_ref[k].astype(F32)
        p = p_ref[...]
        pseudo = p - total / (NX * NH)
        nm = 0.9 * m_ref[...] + pseudo
        new = p - 0.7 * (pseudo + 0.9 * nm)
        nm_ref[...] = nm
        np_ref[...] = new
        s_ref[...] = jnp.broadcast_to(new.astype(BF16)[None], s_ref.shape)

    out = [jax.ShapeDtypeStruct(params.shape, F32)] * 2
    out.append(jax.ShapeDtypeStruct((NH,) + params.shape, BF16))
    return small_call(body, 3, after, out, [], "outer_step")(here, parts, params, moment, *after)


def join_h(here, parts, after):
    _, thin, rows = parts.shape

    def body(here_ref, p_ref, *rest):
        out_ref = rest[len(after)]
        one = p_ref[...].astype(F32).reshape(NH * thin, rows).T.astype(BF16)
        out_ref[...] = jnp.broadcast_to(one[None], out_ref.shape)

    out = [jax.ShapeDtypeStruct((NX, rows, NH * thin), BF16)]
    return small_call(body, 1, after, out, [], "join_h")(here, parts, *after)[0]


def join_x(here, parts, after):
    _, rows, wide = parts.shape

    def body(here_ref, p_ref, *rest):
        out_ref = rest[len(after)]
        for k in range(NX):
            out_ref[:, k * wide : (k + 1) * wide] = p_ref[k]

    out = [jax.ShapeDtypeStruct((rows, NX * wide), BF16)]
    return small_call(body, 1, after, out, [], "join_x")(here, parts, *after)[0]


def on_device(tokens, kv_cotangent, inner_weights, outer_params, outer_momentum):
    tok, cot, w = tokens[0], kv_cotangent[0], inner_weights[0]
    here = jnp.stack([lax.axis_index(a).astype(jnp.int32) for a in ("fsdp", "replica")])

    w_dn = shift_fsdp(w, dy=1)
    w_up = shift_fsdp(w, dy=-1)
    w_z = shift_fsdp(w, dz=1)

    tok_rx = shift_fsdp(tok, dc=1)
    cot_rx = shift_fsdp(cot, dc=1)

    thin = w.shape[1] // (NX * NH)
    parts = w.T.reshape(NX, NH, thin, w.shape[0]).transpose(1, 0, 2, 3)
    parts = parts.reshape(NH, NX * thin, w.shape[0])
    parts = lax.all_to_all(parts, "replica", 0, 0, axis_index_groups=H_GROUPS, tiled=True)

    w_op = shift_fsdp(w_dn, dy=1)
    wz_up = shift_fsdp(w_z, dy=-1)
    wz_dn = shift_fsdp(w_z, dy=1)
    wz_op = shift_fsdp(wz_up, dy=-1)

    g1, g2, g3 = far_gradients(here, tok, tok_rx, cot, cot_rx, (w_dn, w_up))
    r1 = shift_fsdp(g1, dz=1)
    r2 = shift_fsdp(g2, dz=1)
    r3 = shift_fsdp(g3, dz=1)

    sum_h = sum_along_h(here, parts, (g1,))
    total = lax.all_to_all(sum_h, "replica", 0, 0, axis_index_groups=X_GROUPS, tiled=True)

    steps = (0, NY - 1, 1, 2)
    kv_own, grads, to_core, kv_send, own = project(
        here, tok, tok_rx, cot, cot_rx, [w, w_dn, w_up, w_op], steps, after=(sum_h,)
    )

    new_params, new_moment, synced = outer_step(
        here, total, outer_params.T, outer_momentum.T, (own,)
    )
    ready = synced
    synced = lax.all_to_all(synced, "replica", 0, 0, axis_index_groups=H_GROUPS, tiled=True)

    (to_up,) = add_blocks(own, [(3, [(r1, 0)])], BF16, (ready, wz_dn, wz_up))
    two_down = shift_fsdp(to_up, dy=1)

    to_up, to_dn = add_blocks(
        own, [(2, [(r2, 0), (two_down, 0)]), (1, [(r2, 1)])], BF16, ()
    )
    from_dn = shift_fsdp(to_up, dy=1)
    from_up = shift_fsdp(to_dn, dy=-1)

    ready = join_h(here, synced, (to_up,))
    synced = lax.all_to_all(ready, "replica", 0, 0, axis_index_groups=X_GROUPS, tiled=True)

    kv_own, grads, to_core = project(
        here,
        tok,
        tok_rx,
        cot,
        cot_rx,
        [w_z, wz_dn, wz_up, wz_op],
        steps,
        (kv_own, kv_send, grads, to_core),
        after=(ready,),
    )
    other_rx = shift_fsdp(to_core, dc=1)
    keys_values, token_grads = merge(here, kv_own, other_rx, grads, steps, (kv_own,))
    synced = join_x(here, synced, (keys_values,))
    (weight_grads,) = add_blocks(
        own, [(0, [(r3, 0), (from_dn, 0), (from_up, 0)])], F32, (synced,)
    )

    return (
        keys_values[None],
        token_grads[None],
        weight_grads[None],
        new_params.T,
        new_moment.T,
        synced,
    )


def solution(mesh):
    return jax.shard_map(
        on_device,
        mesh=mesh,
        in_specs=(
            P("replica", "fsdp", None),
            P("replica", "fsdp", None),
            P("replica", "fsdp", None),
            P("fsdp", "replica"),
            P("fsdp", "replica"),
        ),
        out_specs=(
            P("replica", "fsdp", None),
            P("replica", "fsdp", None),
            P("replica", "fsdp", None),
            P("fsdp", "replica"),
            P("fsdp", "replica"),
            P("fsdp", None),
        ),
        check_vma=False,
    )
```

```python
import functools

import jax
import jax.numpy as jnp
from jax import lax
from jax.experimental import pallas as pl
from jax.experimental.pallas import tpu as pltpu
from jax.sharding import PartitionSpec as P

NZ, NY, NC = 2, 4, 2
NX, NH = 4, 4
F32, BF16 = jnp.float32, jnp.bfloat16
VMEM_LIMIT = 60 * 1024 * 1024


def shift_fsdp(a, dz=0, dy=0, dc=0):
    pairs = []
    for z in range(NZ):
        for y in range(NY):
            for c in range(NC):
                to = (((z + dz) % NZ) * NY + (y + dy) % NY) * NC + (c + dc) % NC
                pairs.append(((z * NY + y) * NC + c, to))
    return lax.ppermute(a, "fsdp", pairs)


ANY = pl.BlockSpec(memory_space=pl.ANY)
SMEM = pl.BlockSpec(memory_space=pltpu.SMEM)


def place(me):
    return me // (NC * NY), (me // NC) % NY, me % NC


def block_at(z, y, c):
    return (z * NY + y) * NC + c


def columns(ref, b, width=256):
    return ref.at[:, pl.ds(pl.multiple_of(b * width, width), width)]


GRAD_DIMS = (((0,), (0,)), ((), ()))


class Copies:
    def __init__(self, sems):
        self.sems, self.count = sems, 0

    def __call__(self, src, dst):
        c = pltpu.make_async_copy(src, dst, self.sems.at[self.count])
        self.count += 1
        c.start()
        return c


def wait_all(copies):
    for c in copies:
        c.wait()


def far_gradients(here, tok, tok_rx, cot, cot_rx, after):
    rows, kv = cot.shape
    deep = NY * 256

    def body(here_ref, t_ref, tx_ref, c_ref, cx_ref, *rest):
        a_ref, b_ref, d_ref, t_v, tx_v, c_v, cx_v, o_v, sems = rest[len(after) :]
        z, y, core = place(here_ref[0])
        copy = Copies(sems)
        loads = [copy(c_ref, c_v), copy(cx_ref, cx_v)]
        blocks = []
        for k, step in enumerate((2, 1, NY - 1, 0)):
            b = block_at(1 - z, (y + step) % NY, core)
            blocks.append((copy(columns(t_ref, b), columns(t_v, k)), copy(columns(tx_ref, b), columns(tx_v, k))))
        wait_all(loads)
        targets = (a_ref, b_ref.at[pl.ds(0, 256)], b_ref.at[pl.ds(256, 256)], d_ref)
        done = []
        for k in range(NY):
            wait_all(blocks[k])
            at = slice(k * 256, k * 256 + 256)
            acc = lax.dot_general(t_v[:, at], c_v[...], GRAD_DIMS, preferred_element_type=F32)
            acc += lax.dot_general(tx_v[:, at], cx_v[...], GRAD_DIMS, preferred_element_type=F32)
            o_v[at, :] = acc.astype(BF16)
            done.append(copy(o_v.at[pl.ds(k * 256, 256)], targets[k]))
        wait_all(done)

    return pl.pallas_call(
        body,
        in_specs=[SMEM] + [ANY] * (4 + len(after)),
        out_specs=[ANY] * 3,
        out_shape=[jax.ShapeDtypeStruct((m * 256, kv), BF16) for m in (1, 2, 1)],
        scratch_shapes=[
            pltpu.VMEM((rows, deep), BF16),
            pltpu.VMEM((rows, deep), BF16),
            pltpu.VMEM((rows, kv), BF16),
            pltpu.VMEM((rows, kv), BF16),
            pltpu.VMEM((deep, kv), BF16),
            pltpu.SemaphoreType.DMA((3 * NY + 2,)),
        ],
        compiler_params=pltpu.CompilerParams(vmem_limit_bytes=VMEM_LIMIT),
        name="far_gradients",
    )(here, tok, tok_rx, cot, cot_rx, *after)


def add_blocks(own, jobs, dtype, after=(), along=()):
    kv = own.shape[1]
    flat = [(own, k, m) for m, (k, _) in enumerate(jobs)]
    flat += [(a, k, m) for m, (_, others) in enumerate(jobs) for a, k in others]
    n_in = len(flat) + len(after) + len(along)

    def body(*refs):
        ins, outs = refs[: len(flat)], refs[n_in : n_in + len(jobs)]
        for m, o in enumerate(outs):
            acc = ins[m][...]
            for ref, (_, _, job) in zip(ins[len(jobs) :], flat[len(jobs) :]):
                if job == m:
                    acc = acc + ref[...].astype(F32)
            o[...] = acc.astype(dtype)

    def spec(k):
        return pl.BlockSpec((256, kv), lambda i: (k, 0))

    return pl.pallas_call(
        body,
        grid=(1,),
        in_specs=[spec(k) for _, k, _ in flat] + [ANY] * (len(after) + len(along)),
        out_specs=[spec(0) for _ in jobs] + [ANY] * len(along),
        out_shape=[jax.ShapeDtypeStruct((256, kv), dtype) for _ in jobs]
        + [jax.ShapeDtypeStruct(a.shape, a.dtype) for a in along],
        input_output_aliases={len(flat) + len(after) + k: len(jobs) + k for k in range(len(along))},
        compiler_params=pltpu.CompilerParams(vmem_limit_bytes=VMEM_LIMIT),
        name="add_blocks",
    )(*[a for a, _, _ in flat], *after, *along)


def project(here, tok, tok_rx, cot, cot_rx, pieces, steps, before=None, after=()):
    rows, d = tok.shape
    kv = cot.shape[1]
    far = before is not None
    n_w = len(pieces)
    deep = NY * 256

    def body(here_ref, t_ref, tx_ref, c_ref, cx_ref, *rest):
        w_refs, rest = rest[:n_w], rest[n_w:]
        if far:
            own_in, send_in = rest[:2]
            rest = rest[4 + len(after) :]
            own_ref, tg_ref, out_ref = rest[:3]
            w_v, t_v, tr_v, c_v, cr_v, g_v, own_v, send_v, out_v, sems = rest[3:]
        else:
            rest = rest[len(after) :]
            own_ref, tg_ref, out_ref, send_ref, grad_ref = rest[:5]
            w_v, t_v, tr_v, c_v, cr_v, g_v, own_v, send_v, out_v, grad_v, sems = rest[5:]
        z, y, core = place(here_ref[0])
        zz = 1 - z if far else z
        ys = [(y + step) % NY for step in steps]
        count = [0]

        def copy(src, dst):
            c = pltpu.make_async_copy(src, dst, sems.at[count[0]])
            count[0] += 1
            c.start()
            return c

        ready_c = copy(c_ref, c_v)
        ready_w = [copy(r, w_v.at[pl.ds(k * 256, 256)]) for k, r in enumerate(w_refs)]
        ready_t = [copy(columns(t_ref, block_at(zz, yy, core)), columns(t_v, k)) for k, yy in enumerate(ys)]
        ready_cr = copy(cx_ref, cr_v)
        ready_tr = [copy(columns(tx_ref, block_at(zz, yy, core)), columns(tr_v, k)) for k, yy in enumerate(ys)]
        if far:
            ready_own = copy(own_in, own_v)
            ready_send = copy(send_in, send_v)
        done = []
        trans = (((1,), (1,)), ((), ()))
        ready_c.wait()
        for k in range(NY):
            ready_w[k].wait()
            at = slice(k * 256, k * 256 + 256)
            g_v[:, at] = lax.dot_general(
                c_v[...], w_v[at, :], trans, preferred_element_type=F32
            ).astype(BF16)
            done.append(copy(columns(g_v, k), columns(tg_ref, block_at(zz, ys[k], core))))
        for c in ready_t:
            c.wait()
        sums = jnp.dot(t_v[...], w_v[...], preferred_element_type=F32)
        if far:
            ready_own.wait()
            sums += own_v[...]
        own_v[...] = sums
        done.append(copy(own_v, own_ref))
        ready_cr.wait()
        out_v[:, :deep] = lax.dot_general(
            cr_v[...], w_v[...], trans, preferred_element_type=F32
        ).astype(BF16)
        for c in ready_tr:
            c.wait()
        sums = jnp.dot(tr_v[...], w_v[...], preferred_element_type=F32)
        if far:
            ready_send.wait()
            out_v[:, deep:] = (send_v[...] + sums).astype(BF16)
            done.append(copy(out_v, out_ref.at[:, pl.ds(deep, deep + kv)]))
        else:
            done.append(copy(out_v, out_ref.at[:, pl.ds(0, deep)]))
            send_v[...] = sums
            done.append(copy(send_v, send_ref))
            for k in range(NY):
                at = slice(k * 256, k * 256 + 256)
                acc = lax.dot_general(t_v[:, at], c_v[...], GRAD_DIMS, preferred_element_type=F32)
                acc += lax.dot_general(tr_v[:, at], cr_v[...], GRAD_DIMS, preferred_element_type=F32)
                grad_v[at, :] = acc
                done.append(copy(grad_v.at[pl.ds(k * 256, 256)], grad_ref.at[pl.ds(k * 256, 256)]))
        for c in done:
            c.wait()

    sums = jax.ShapeDtypeStruct((rows, kv), F32)
    out_shape = [
        sums,
        jax.ShapeDtypeStruct((rows, d), BF16),
        jax.ShapeDtypeStruct((rows, 2 * deep + kv), BF16),
    ]
    args = [here, tok, tok_rx, cot, cot_rx, *pieces]
    alias = {}
    scratch = [
        pltpu.VMEM((deep, kv), BF16),
        pltpu.VMEM((rows, deep), BF16),
        pltpu.VMEM((rows, deep), BF16),
        pltpu.VMEM((rows, kv), BF16),
        pltpu.VMEM((rows, kv), BF16),
        pltpu.VMEM((rows, deep), BF16),
        pltpu.VMEM((rows, kv), F32),
        pltpu.VMEM((rows, kv), F32),
        pltpu.VMEM((rows, deep + (kv if far else 0)), BF16),
    ]
    if far:
        own, send, grads_in, out_in = before
        alias = {len(args) + 2: 1, len(args) + 3: 2}
        args += [own, send, grads_in, out_in]
    else:
        gradient = jax.ShapeDtypeStruct((deep, kv), F32)
        out_shape += [sums, gradient]
        scratch.append(pltpu.VMEM(gradient.shape, F32))
    args += list(after)
    return pl.pallas_call(
        body,
        in_specs=[SMEM] + [ANY] * (len(args) - 1),
        out_specs=[ANY] * len(out_shape),
        out_shape=out_shape,
        scratch_shapes=scratch + [pltpu.SemaphoreType.DMA((32,))],
        input_output_aliases=alias,
        compiler_params=pltpu.CompilerParams(vmem_limit_bytes=VMEM_LIMIT),
        name="project",
    )(*args)


def merge(here, own, other_rx, grads, steps, after):
    rows, kv = own.shape
    deep = NY * 256

    def body(here_ref, own_ref, a_ref, _, *rest):
        kv_ref, tg_ref, own_v, a_v, kv_v, sems = rest[len(after) :]
        z, y, core = place(here_ref[0])
        count = [0]

        def copy(src, dst):
            c = pltpu.make_async_copy(src, dst, sems.at[count[0]])
            count[0] += 1
            c.start()
            return c

        load_kv = copy(a_ref.at[:, pl.ds(2 * deep, kv)], a_v.at[:, pl.ds(2 * deep, kv)])
        load_own = copy(own_ref, own_v)
        loads = [copy(columns(a_ref, k), columns(a_v, k)) for k in range(2 * NY)]
        out = []
        for k, load in enumerate(loads):
            load.wait()
            zz = z if k < NY else 1 - z
            at = block_at(zz, (y + steps[k % NY]) % NY, 1 - core)
            out.append(copy(columns(a_v, k), columns(tg_ref, at)))
        load_kv.wait()
        load_own.wait()
        kv_v[...] = (own_v[...] + a_v[:, 2 * deep :].astype(F32)).astype(BF16)
        out.append(copy(kv_v, kv_ref))
        for c in out:
            c.wait()

    return pl.pallas_call(
        body,
        in_specs=[SMEM] + [ANY] * (3 + len(after)),
        out_specs=[ANY, ANY],
        out_shape=[
            jax.ShapeDtypeStruct((rows, kv), BF16),
            jax.ShapeDtypeStruct(grads.shape, BF16),
        ],
        scratch_shapes=[
            pltpu.VMEM((rows, kv), F32),
            pltpu.VMEM(other_rx.shape, BF16),
            pltpu.VMEM((rows, kv), BF16),
            pltpu.SemaphoreType.DMA((4 * NY + 3,)),
        ],
        input_output_aliases={3: 1},
        compiler_params=pltpu.CompilerParams(vmem_limit_bytes=VMEM_LIMIT),
        name="merge",
    )(here, own, other_rx, grads, *after)


WHOLE = pl.BlockSpec(memory_space=pltpu.VMEM)


def small_call(body, n_in, after, out_shape, scratch, name):
    return pl.pallas_call(
        body,
        in_specs=[SMEM] + [WHOLE] * n_in + [ANY] * len(after),
        out_specs=[WHOLE] * len(out_shape),
        out_shape=out_shape,
        scratch_shapes=scratch,
        compiler_params=pltpu.CompilerParams(vmem_limit_bytes=VMEM_LIMIT),
        name=name,
    )


X_GROUPS = [[x * NH + h for x in range(NX)] for h in range(NH)]
H_GROUPS = [[x * NH + h for h in range(NH)] for x in range(NX)]


def sum_along_h(here, parts, after):
    _, wide, rows = parts.shape

    def body(here_ref, p_ref, *rest):
        out_ref = rest[len(after)]
        acc = p_ref[0].astype(F32)
        for k in range(1, NH):
            acc += p_ref[k].astype(F32)
        out_ref[...] = acc.astype(BF16).reshape(out_ref.shape)

    out = [jax.ShapeDtypeStruct((NX, wide // NX, rows), BF16)]
    return small_call(body, 1, after, out, [], "sum_along_h")(here, parts, *after)[0]


def outer_step(here, parts, params, moment, after):
    def body(here_ref, t_ref, p_ref, m_ref, *rest):
        np_ref, nm_ref, s_ref = rest[len(after) :]
        total = t_ref[0].astype(F32)
        for k in range(1, NX):
            total += t_ref[k].astype(F32)
        p = p_ref[...]
        pseudo = p - total / (NX * NH)
        nm = 0.9 * m_ref[...] + pseudo
        new = p - 0.7 * (pseudo + 0.9 * nm)
        nm_ref[...] = nm
        np_ref[...] = new
        s_ref[...] = jnp.broadcast_to(new.astype(BF16)[None], s_ref.shape)

    out = [jax.ShapeDtypeStruct(params.shape, F32)] * 2
    out.append(jax.ShapeDtypeStruct((NH,) + params.shape, BF16))
    return small_call(body, 3, after, out, [], "outer_step")(here, parts, params, moment, *after)


def join_h(here, parts, after):
    _, thin, rows = parts.shape

    def body(here_ref, p_ref, *rest):
        out_ref = rest[len(after)]
        one = p_ref[...].astype(F32).reshape(NH * thin, rows).T.astype(BF16)
        out_ref[...] = jnp.broadcast_to(one[None], out_ref.shape)

    out = [jax.ShapeDtypeStruct((NX, rows, NH * thin), BF16)]
    return small_call(body, 1, after, out, [], "join_h")(here, parts, *after)[0]


def join_x(here, parts, after):
    _, rows, wide = parts.shape

    def body(here_ref, p_ref, *rest):
        out_ref = rest[len(after)]
        for k in range(NX):
            out_ref[:, k * wide : (k + 1) * wide] = p_ref[k]

    out = [jax.ShapeDtypeStruct((rows, NX * wide), BF16)]
    return small_call(body, 1, after, out, [], "join_x")(here, parts, *after)[0]


def on_device(tokens, kv_cotangent, inner_weights, outer_params, outer_momentum):
    tok, cot, w = tokens[0], kv_cotangent[0], inner_weights[0]
    here = jnp.stack([lax.axis_index(a).astype(jnp.int32) for a in ("fsdp", "replica")])

    w_dn = shift_fsdp(w, dy=1)
    w_up = shift_fsdp(w, dy=-1)
    w_z = shift_fsdp(w, dz=1)

    tok_rx = shift_fsdp(tok, dc=1)
    cot_rx = shift_fsdp(cot, dc=1)

    thin = w.shape[1] // (NX * NH)
    parts = w.T.reshape(NX, NH, thin, w.shape[0]).transpose(1, 0, 2, 3)
    parts = parts.reshape(NH, NX * thin, w.shape[0])
    parts = lax.all_to_all(parts, "replica", 0, 0, axis_index_groups=H_GROUPS, tiled=True)

    w_op = shift_fsdp(w_dn, dy=1)
    wz_up = shift_fsdp(w_z, dy=-1)
    wz_dn = shift_fsdp(w_z, dy=1)
    wz_op = shift_fsdp(wz_up, dy=-1)

    g1, g2, g3 = far_gradients(here, tok, tok_rx, cot, cot_rx, (w_dn, w_up))
    r1 = shift_fsdp(g1, dz=1)
    r2 = shift_fsdp(g2, dz=1)
    r3 = shift_fsdp(g3, dz=1)

    sum_h = sum_along_h(here, parts, (g1,))
    total = lax.all_to_all(sum_h, "replica", 0, 0, axis_index_groups=X_GROUPS, tiled=True)

    steps = (0, NY - 1, 1, 2)
    kv_own, grads, to_core, kv_send, own = project(
        here, tok, tok_rx, cot, cot_rx, [w, w_dn, w_up, w_op], steps, after=(sum_h,)
    )

    new_params, new_moment, synced = outer_step(
        here, total, outer_params.T, outer_momentum.T, (own,)
    )
    ready = synced
    synced = lax.all_to_all(synced, "replica", 0, 0, axis_index_groups=H_GROUPS, tiled=True)

    (to_up,) = add_blocks(own, [(3, [(r1, 0)])], BF16, (ready, wz_dn, wz_up))
    two_down = shift_fsdp(to_up, dy=1)

    to_up, to_dn = add_blocks(
        own, [(2, [(r2, 0), (two_down, 0)]), (1, [(r2, 1)])], BF16, ()
    )
    from_dn = shift_fsdp(to_up, dy=1)
    from_up = shift_fsdp(to_dn, dy=-1)

    ready = join_h(here, synced, (to_up,))
    synced = lax.all_to_all(ready, "replica", 0, 0, axis_index_groups=X_GROUPS, tiled=True)

    kv_own, grads, to_core = project(
        here,
        tok,
        tok_rx,
        cot,
        cot_rx,
        [w_z, wz_dn, wz_up, wz_op],
        steps,
        (kv_own, kv_send, grads, to_core),
        after=(ready,),
    )
    other_rx = shift_fsdp(to_core, dc=1)
    keys_values, token_grads = merge(here, kv_own, other_rx, grads, steps, (kv_own,))
    synced = join_x(here, synced, (keys_values,))
    (weight_grads,) = add_blocks(
        own, [(0, [(r3, 0), (from_dn, 0), (from_up, 0)])], F32, (synced,)
    )

    return (
        keys_values[None],
        token_grads[None],
        weight_grads[None],
        new_params.T,
        new_moment.T,
        synced,
    )


def solution(mesh):
    return jax.shard_map(
        on_device,
        mesh=mesh,
        in_specs=(
            P("replica", "fsdp", None),
            P("replica", "fsdp", None),
            P("replica", "fsdp", None),
            P("fsdp", "replica"),
            P("fsdp", "replica"),
        ),
        out_specs=(
            P("replica", "fsdp", None),
            P("replica", "fsdp", None),
            P("replica", "fsdp", None),
            P("fsdp", "replica"),
            P("fsdp", "replica"),
            P("fsdp", None),
        ),
        check_vma=False,
    )
```
